32 devices in a mesh: parts: 2 (over y), band: 16 (over z, x, core).
Axes of the slice: x: 2, y: 2, z: 4, core: 2. Of those that a mesh axis runs over, the one named last changes fastest.
Arguments:
- grid_nodes: bfloat16 [16384, 512], P(('parts', 'band')), parts along dimension 0, may hold values from -6 to 6
- mesh_nodes: bfloat16 [2048, 512], P(('parts', 'band')), parts along dimension 0, may hold values from -6 to 6
- weights: bfloat16 [3, 6, 512, 512], replicated, may hold values from -0.25 to 0.25
- raw_weights: float32 [3, 4, 512], replicated, may hold values from -3 to 3
- enc_raw: float32 [4, 12288], P(None, 'band'), may hold values from -6 to 6
- enc_src: int32 [12288], P('band'), may hold values from 0 to 767, as said below
- enc_dst: int32 [12288], P('band'), may hold values from 0 to 63
- enc_count: int32 [16], P('band'), may hold values from 576 to 768, as said below
- enc_send: int32 [16, 256], P('band'), may hold values from 0 to 511, as said below
- proc_raw: float32 [4, 8192], P(None, 'band'), may hold values from -6 to 6
- proc_src: int32 [8192], P('band'), may hold values from 0 to 319, as said below
- proc_dst: int32 [8192], P('band'), may hold values from 0 to 63
- proc_count: int32 [16], P('band'), may hold values from 384 to 512, as said below
- proc_send: int32 [16, 16, 16], P('band'), may hold values from 0 to 63, as said below
- dec_raw: float32 [4, 24576], P(None, 'band'), may hold values from -6 to 6
- dec_src: int32 [24576], P('band'), may hold values from 0 to 95, as said below
- dec_send: int32 [16, 32], P('band'), may hold values from 0 to 63, as said below
Outputs:
- grid_out: bfloat16 [16384, 512], P(('parts', 'band')), parts along dimension 0
- mesh_out: bfloat16 [2048, 512], P(('parts', 'band')), parts along dimension 0
The draws below stay inside these ranges and needn't reach their ends.
There are 2 independent parts, one for each index of `parts`. The reference program is written for one: setup_inputs(seed, part) draws one part's arguments, and reference() takes and returns one part's arrays. A program takes and returns all parts, laid end to end along the dimension named above; an argument that names none is the same for every part. Nothing has to cross between parts.
Inputs may be any that keep to these rules, and one draw needn't show every extreme that they name: `enc_src`: values index a band's grid-to-mesh table of 768 rows; the first band never takes values below 128, the last band never values of 640 or more. `enc_count`: live slots of each band; some band is full in every draw. `enc_send`: each band's 128 + 128 rows are distinct local grid rows. `proc_src`: values index a band's mesh table; with k = value - 64 >= 0, k // 16 is another band, and if that band is not adjacent then k % 16 < 2. `proc_count`: live slots of each band; some band is full in every draw. `proc_send`: each entry [a, b] holds 16 distinct local mesh rows of band a. `dec_src`: values index a band's mesh-to-grid table of 96 rows; the first band never takes values below 16, the last band never values of 80 or more. `dec_send`: each band's 16 + 16 rows are distinct local mesh rows.
All inputs are finite; a program needn't handle non-finite values.
Results may differ from the reference program's by a relative error of at most 0.012.
Values may be sent and summed in bfloat16 or wider, within the bound.
A program may use at most 64 MiB of HBM per device.

```python
import jax
import jax.numpy as jnp
from jax import lax

D = 512
GRID_DEV = 512
FEATS = 4
CAP_NEAR = 16
CAP_FAR = 2
BANDS = 16
MESH_DEV = 64
CAPG = 128
CAPD = 16
ENC_SLOTS = 768
PROC_SLOTS = 512
DEC_SLOTS = 1536
GRID = 8192
MESH = 1024
ENC_EDGES = 12288
PROC_EDGES = 8192
DEC_EDGES = 24576
N_BAND = 16


def live_counts(key, slot_count, salt):
    key = jax.random.fold_in(key, salt)
    leading, second = jax.random.split(key)
    counts = jax.random.randint(leading, (BANDS,), 3 * slot_count // 4, slot_count + 1)
    full_band = jax.random.randint(second, (), 0, BANDS)
    return counts.at[full_band].set(slot_count).astype(jnp.int32)


def distinct_rows(key, leading_shape, row_count, taken):
    scores = jax.random.randint(key, leading_shape + (row_count,), 0, 2 ** 16) * row_count + jnp.arange(row_count, dtype=jnp.int32)
    return jnp.argsort(scores, axis=-1)[..., :taken].astype(jnp.int32)


def rim_pick(key, slot_count, rim_cap, row_count):
    key_cross, key_side, key_rim, key_own = jax.random.split(key, 4)
    band_index = jnp.arange(BANDS, dtype=jnp.int32)[:, None]
    cross = jax.random.randint(key_cross, (BANDS, slot_count), 0, 4) == 0
    upward = jax.random.randint(key_side, (BANDS, slot_count), 0, 2) == 1
    upward = jnp.where(band_index == 0, True, jnp.where(band_index == BANDS - 1, False, upward))
    rim_slot = jax.random.randint(key_rim, (BANDS, slot_count), 0, rim_cap)
    own_rows = jax.random.randint(key_own, (BANDS, slot_count), 0, row_count)
    picked = jnp.where(cross, jnp.where(upward, rim_cap + row_count + rim_slot, rim_slot), rim_cap + own_rows)
    picked = picked.at[0, 0].set(2 * rim_cap + row_count - 1).at[1, 0].set(0)
    return picked.reshape(-1).astype(jnp.int32)


def draw_enc_count(key, part):
    return live_counts(key, ENC_SLOTS, 101)


def draw_proc_count(key, part):
    return live_counts(key, PROC_SLOTS, 102)


def draw_enc_src(key, part):
    key = jax.random.fold_in(key, 7)
    return rim_pick(key, ENC_SLOTS, CAPG, GRID_DEV)


def draw_dec_src(key, part):
    key = jax.random.fold_in(key, 8)
    return rim_pick(key, DEC_SLOTS, CAPD, MESH_DEV)


def draw_enc_send(key, part):
    key = jax.random.fold_in(key, 10)
    return distinct_rows(key, (BANDS,), GRID_DEV, 2 * CAPG)


def draw_dec_send(key, part):
    key = jax.random.fold_in(key, 11)
    return distinct_rows(key, (BANDS,), MESH_DEV, 2 * CAPD)


def draw_proc_send(key, part):
    key = jax.random.fold_in(key, 12)
    return distinct_rows(key, (BANDS, BANDS), MESH_DEV, CAP_NEAR)


def draw_proc_src(key, part):
    counts = live_counts(key, PROC_SLOTS, 102)
    key = jax.random.fold_in(key, 9)
    key_pick, key_local, key_coin, key_order = jax.random.split(key, 4)
    slot_total = BANDS * CAP_NEAR
    flat = jnp.arange(slot_total, dtype=jnp.int32)
    peer_band = flat // CAP_NEAR
    slot_index = flat % CAP_NEAR
    band_index = jnp.arange(BANDS, dtype=jnp.int32)[:, None]
    distance = jnp.abs(peer_band[None, :] - band_index)
    usable = (distance == 1) | (distance > 1) & (slot_index[None, :] < CAP_FAR)
    ordering = jnp.argsort((~usable).astype(jnp.int32), axis=1, stable=True).astype(jnp.int32)
    needed = jnp.sum(usable.astype(jnp.int32), axis=1)
    slots = jnp.arange(PROC_SLOTS, dtype=jnp.int32)[None, :]
    pick_remote = jax.random.randint(key_pick, (BANDS, PROC_SLOTS), 0, needed[:, None])
    remote = MESH_DEV + jnp.take_along_axis(ordering, pick_remote, axis=1)
    required = MESH_DEV + jnp.take_along_axis(ordering, jnp.broadcast_to(jnp.clip(slots, 0, slot_total - 1), (BANDS, PROC_SLOTS)), axis=1)
    local_rows = jax.random.randint(key_local, (BANDS, PROC_SLOTS), 0, MESH_DEV)
    coin = jax.random.randint(key_coin, (BANDS, PROC_SLOTS), 0, 2)
    base = jnp.where(slots < needed[:, None], required, jnp.where(coin == 0, local_rows, remote))
    scores = jnp.where(slots < counts[:, None], jax.random.randint(key_order, (BANDS, PROC_SLOTS), 0, 2 ** 16) * PROC_SLOTS + slots, 2 ** 28 + slots)
    shuffle = jnp.argsort(scores, axis=1)
    return jnp.take_along_axis(base, shuffle, axis=1).reshape(-1).astype(jnp.int32)


def touch_ends(drawn, own_key, smallest, top_value):
    index_at = [jax.random.randint(jax.random.fold_in(own_key, axis), (), 0, length) for axis, length in enumerate(drawn.shape)]
    main_axis = drawn.shape.index(max(drawn.shape))
    beside = index_at[:main_axis] + [(index_at[main_axis] + 1) % drawn.shape[main_axis]] + index_at[main_axis + 1:]
    return drawn.at[tuple(index_at)].set(smallest).at[tuple(beside)].set(top_value)


def levels(own_key, extent, pieces, least, largest):
    def one(dim, shards_of):
        heights = jax.random.uniform(jax.random.fold_in(jax.random.fold_in(own_key, 6), dim), (shards_of,), jnp.float32, least / len(pieces), largest / len(pieces))
        return jnp.repeat(jnp.exp(heights), extent[dim] // shards_of).reshape((-1,) + (1,) * (len(extent) - dim - 1))

    loudness = one(*pieces[0])
    for cut in pieces[1:]:
        loudness = loudness * one(*cut)
    return loudness


def gaussian(own_key, shape, deviation, reach, cuts=(), kind=jnp.bfloat16):
    factor_of = levels(own_key, shape, cuts, -0.22, 0.18) if cuts else 1.0
    drawn = jax.random.normal(own_key, shape, jnp.float32) * deviation * factor_of
    return jnp.minimum(jnp.maximum(drawn, -reach), reach).astype(kind)


def setup_inputs(seed: int = 0, part: int = 0) -> dict:
    key_of = jax.random.split(jax.random.key(seed), 18)
    part_splits = jax.random.split(jax.random.fold_in(key_of[17], part), 18)
    return {
        "grid_nodes": gaussian(part_splits[0], (GRID, D), 1.0, 6.0, ((0, 16),)),
        "mesh_nodes": gaussian(part_splits[1], (MESH, D), 1.0, 6.0, ((0, 16),)),
        "weights": gaussian(key_of[2], (3, 6, D, D), D ** -0.5, 0.25),
        "raw_weights": gaussian(key_of[3], (3, FEATS, D), 0.5, 3.0, (), jnp.float32),
        "enc_raw": gaussian(key_of[4], (FEATS, ENC_EDGES), 1.0, 6.0, ((1, 16),), jnp.float32),
        "enc_src": draw_enc_src(jax.random.fold_in(key_of[17], 71), part),
        "enc_dst": touch_ends(jax.random.randint(key_of[6], (ENC_EDGES,), 0, MESH_DEV), jax.random.fold_in(key_of[6], 1), 0, MESH_DEV - 1).astype(jnp.int32),
        "enc_count": draw_enc_count(jax.random.fold_in(key_of[17], 71), part),
        "enc_send": draw_enc_send(jax.random.fold_in(key_of[17], 71), part),
        "proc_raw": gaussian(key_of[9], (FEATS, PROC_EDGES), 1.0, 6.0, ((1, 16),), jnp.float32),
        "proc_src": draw_proc_src(jax.random.fold_in(key_of[17], 71), part),
        "proc_dst": touch_ends(jax.random.randint(key_of[11], (PROC_EDGES,), 0, MESH_DEV), jax.random.fold_in(key_of[11], 1), 0, MESH_DEV - 1).astype(jnp.int32),
        "proc_count": draw_proc_count(jax.random.fold_in(key_of[17], 71), part),
        "proc_send": draw_proc_send(jax.random.fold_in(key_of[17], 71), part),
        "dec_raw": gaussian(key_of[14], (FEATS, DEC_EDGES), 1.0, 6.0, ((1, 16),), jnp.float32),
        "dec_src": draw_dec_src(jax.random.fold_in(key_of[17], 71), part),
        "dec_send": draw_dec_send(jax.random.fold_in(key_of[17], 71), part),
    }


def layer_norm(values):
    average = lax.optimization_barrier(jnp.mean(values, axis=-1, keepdims=True))
    centred = values - average
    return centred * lax.rsqrt(lax.optimization_barrier(jnp.mean(centred * centred, axis=-1, keepdims=True)) + 1e-05)

def raw_term(raw_feats, raw_w):
    return lax.dot_general(raw_feats, raw_w, (((0,), (0,)), ((), ())), precision=lax.Precision.HIGHEST, preferred_element_type=jnp.float32)

def edge_out(pre_act, edge_w):
    hidden = jax.nn.silu(pre_act).astype(jnp.bfloat16)
    return layer_norm(jnp.dot(hidden, edge_w, preferred_element_type=jnp.float32)).astype(jnp.bfloat16)

def node_update(nodes, agg_rows, w_self, w_agg, w_out):
    inner_sum = jnp.dot(nodes, w_self, preferred_element_type=jnp.float32) + jnp.dot(agg_rows, w_agg, preferred_element_type=jnp.float32)
    hidden = jax.nn.silu(inner_sum).astype(jnp.bfloat16)
    return (nodes.astype(jnp.float32) + layer_norm(jnp.dot(hidden, w_out, preferred_element_type=jnp.float32))).astype(jnp.bfloat16)

def rim_source(local_idx, send_rows, rim_cap, row_count):
    band_total = send_rows.shape[0]
    band_index = jnp.arange(band_total, dtype=jnp.int32)[:, None]
    below = jnp.maximum(band_index - 1, 0)
    above = jnp.minimum(band_index + 1, band_total - 1)
    from_below = jnp.take_along_axis(send_rows[below[:, 0]], rim_cap + jnp.clip(local_idx, 0, rim_cap - 1), axis=1)
    from_above = jnp.take_along_axis(send_rows[above[:, 0]], jnp.clip(local_idx - rim_cap - row_count, 0, rim_cap - 1), axis=1)
    own_rows = band_index * row_count + jnp.clip(local_idx - rim_cap, 0, row_count - 1)
    picked = jnp.where(local_idx < rim_cap, below * row_count + from_below, jnp.where(local_idx < rim_cap + row_count, own_rows, above * row_count + from_above))
    return picked.astype(jnp.int32)

def band_raw(raw_feats, slot_count):
    return raw_feats.reshape(FEATS, N_BAND, slot_count).transpose(1, 0, 2)

def mesh_aggregate(src_proj, dst_proj, raw_w, edge_w, global_src, local_dst, raw_feats, live_count):
    dst_bands = dst_proj.reshape(N_BAND, MESH_DEV, -1)

    def one_band(items):
        sources, targets, raw_part, limit, dst_rows = items
        pre_act = src_proj[sources].astype(jnp.float32) + dst_rows[targets] + raw_term(raw_part, raw_w)
        message = edge_out(pre_act, edge_w)
        live = jnp.arange(sources.shape[0], dtype=jnp.int32) < limit
        onehot = ((targets[None, :] == jnp.arange(MESH_DEV, dtype=jnp.int32)[:, None]) & live[None, :]).astype(jnp.bfloat16)
        return jnp.dot(onehot, message, preferred_element_type=jnp.float32)
    summed = lax.map(one_band, (global_src, local_dst, raw_feats, live_count, dst_bands))
    return summed.reshape(N_BAND * MESH_DEV, -1).astype(jnp.bfloat16)

def reference(grid_nodes, mesh_nodes, weights, raw_weights, enc_raw, enc_src, enc_dst, enc_count, enc_send, proc_raw, proc_src, proc_dst, proc_count, proc_send, dec_raw, dec_src, dec_send):
    grid_proj = jnp.dot(grid_nodes, weights[0, 0], preferred_element_type=jnp.float32).astype(jnp.bfloat16)
    mesh_dst = jnp.dot(mesh_nodes, weights[0, 1], preferred_element_type=jnp.float32)
    enc_global = rim_source(enc_src.reshape(N_BAND, -1), enc_send, CAPG, GRID_DEV)
    enc_agg = mesh_aggregate(grid_proj, mesh_dst, raw_weights[0], weights[0, 2], enc_global, enc_dst.reshape(N_BAND, -1), band_raw(enc_raw, ENC_SLOTS), enc_count)
    mesh_one = node_update(mesh_nodes, enc_agg, weights[0, 3], weights[0, 4], weights[0, 5])
    mesh_proj = jnp.dot(mesh_one, weights[1, 0], preferred_element_type=jnp.float32).astype(jnp.bfloat16)
    proc_dst_proj = jnp.dot(mesh_one, weights[1, 1], preferred_element_type=jnp.float32)
    local_idx = proc_src.reshape(N_BAND, -1)
    band_index = jnp.arange(N_BAND, dtype=jnp.int32)[:, None]
    offset = local_idx - MESH_DEV
    peer_band = jnp.clip(offset // CAP_NEAR, 0, N_BAND - 1).astype(jnp.int32)
    slot_index = jnp.clip(offset - peer_band * CAP_NEAR, 0, CAP_NEAR - 1).astype(jnp.int32)
    sent_rows = proc_send[peer_band, jnp.broadcast_to(band_index, local_idx.shape), slot_index]
    proc_global = jnp.where(local_idx < MESH_DEV, band_index * MESH_DEV + local_idx, peer_band * MESH_DEV + sent_rows).astype(jnp.int32)
    proc_agg = mesh_aggregate(mesh_proj, proc_dst_proj, raw_weights[1], weights[1, 2], proc_global, proc_dst.reshape(N_BAND, -1), band_raw(proc_raw, PROC_SLOTS), proc_count)
    mesh_out = node_update(mesh_one, proc_agg, weights[1, 3], weights[1, 4], weights[1, 5])
    dec_proj = jnp.dot(mesh_out, weights[2, 0], preferred_element_type=jnp.float32).astype(jnp.bfloat16)
    dec_global = rim_source(dec_src.reshape(N_BAND, -1), dec_send, CAPD, MESH_DEV)
    grid_bands = grid_nodes.reshape(N_BAND, GRID_DEV, -1)

    def decode_band(items):
        sources, raw_part, grid_rows = items
        grid_dst = jnp.dot(grid_rows, weights[2, 1], preferred_element_type=jnp.float32)
        width = grid_dst.shape[1]
        pre_act = dec_proj[sources].astype(jnp.float32).reshape(GRID_DEV, 3, width) + grid_dst[:, None, :] + raw_term(raw_part, raw_weights[2]).reshape(GRID_DEV, 3, width)
        message = edge_out(pre_act.reshape(-1, width), weights[2, 2])
        dec_agg = lax.optimization_barrier(jnp.sum(message.astype(jnp.float32).reshape(GRID_DEV, 3, width), axis=1)).astype(jnp.bfloat16)
        return node_update(grid_rows, dec_agg, weights[2, 3], weights[2, 4], weights[2, 5])
    grid_out = lax.map(decode_band, (dec_global, band_raw(dec_raw, DEC_SLOTS), grid_bands))
    return (grid_out.reshape(N_BAND * GRID_DEV, -1), mesh_out)
```

```python
import functools

import jax
import jax.numpy as jnp
from jax import lax
from jax.experimental import pallas as pl
from jax.experimental.pallas import tpu as pltpu
from jax.sharding import PartitionSpec as P

BF = jnp.bfloat16
F32 = jnp.float32
MESH_ID = pl.DeviceIdType.MESH


def dot(a, b):
    return jnp.dot(a, b, preferred_element_type=F32)


def dot_t(a, b):
    return lax.dot_general(a, b, (((0,), (0,)), ((), ())), preferred_element_type=F32)


def silu(x):
    half = 0.5 * x
    return (half + half * jnp.tanh(half)).astype(BF)


def layer_norm(values):
    average = jnp.mean(values, axis=-1, keepdims=True)
    centred = values - average
    return centred * lax.rsqrt(jnp.mean(centred * centred, axis=-1, keepdims=True) + 1e-05)


def onehot_t(index_row, rows):
    lanes = index_row.shape[1]
    return (lax.broadcasted_iota(jnp.int32, (rows, lanes), 0) == index_row).astype(F32).astype(BF)


def split(x):
    high = x.astype(BF)
    return high, (x - high.astype(F32)).astype(BF)


def raw_rows(raw, pad):
    high, low = split(raw)
    rest = jnp.zeros((pad - 3 * raw.shape[0], raw.shape[1]), F32)
    return jnp.concatenate([high.astype(F32), low.astype(F32), high.astype(F32), rest], axis=0).astype(BF)


def raw_table(raw_w, pad):
    high, low = split(raw_w)
    rest = jnp.zeros((pad - 3 * raw_w.shape[0], raw_w.shape[1]), F32)
    return jnp.concatenate([high.astype(F32), high.astype(F32), low.astype(F32), rest], axis=0).astype(BF)


def kernel(
    n,
    far_rows,
    grid_hbm,
    mesh_ref,
    w_hbm,
    raww_ref,
    enc_raw_ref,
    enc_src_ref,
    enc_dst_ref,
    enc_count_ref,
    enc_send_ref,
    proc_raw_ref,
    proc_src_ref,
    proc_dst_ref,
    proc_count_ref,
    proc_send_ref,
    dec_raw_ref,
    dec_src_ref,
    dec_send_ref,
    grid_out_hbm,
    mesh_out_ref,
    grid_ref,
    w_ref,
    enc_table,
    enc_out,
    enc_pre,
    proc_table,
    proc_near_out,
    far_out,
    far_in,
    dec_table,
    dec_near_out,
    grid_dst,
    grid_self,
    out_buf,
    w_sem,
    grid_sem,
    out_sem,
    halo_send,
    halo_recv,
    far_send_sem,
    far_recv_sem,
):
    me = lax.axis_index("band")
    part = lax.axis_index("parts")
    grid_rows = grid_ref.shape[0]
    width = grid_ref.shape[1]
    mesh_rows = mesh_ref.shape[0]
    enc_edges = enc_src_ref.shape[1]
    proc_edges = proc_src_ref.shape[1]
    cap_g = enc_send_ref.shape[1] // 2
    cap_d = dec_send_ref.shape[1] // 2
    near = proc_send_ref.shape[2]
    has_below = me > 0
    has_above = me < n - 1

    grid_copy = pltpu.make_async_copy(grid_hbm, grid_ref, grid_sem)
    grid_copy.start()

    def w_copy(k, m):
        return pltpu.make_async_copy(w_hbm.at[k, m], w_ref.at[k, m], w_sem.at[k, m])

    w_copy(0, 0).start()

    enc_table[pl.ds(0, cap_g), :] = jnp.zeros((cap_g, width), BF)
    enc_table[pl.ds(cap_g + grid_rows, cap_g), :] = jnp.zeros((cap_g, width), BF)
    proc_table[...] = jnp.zeros(proc_table.shape, BF)
    far_in[...] = jnp.zeros(far_in.shape, F32)
    dec_table[...] = jnp.zeros(dec_table.shape, BF)

    barrier = pltpu.get_barrier_semaphore()

    def greet(d, carry):
        pl.semaphore_signal(
            barrier, inc=1, device_id=(part, lax.rem(me + d, n)), device_id_type=MESH_ID
        )
        return carry

    lax.fori_loop(1, n, greet, 0)

    order = [
        (0, 1), (0, 2), (2, 1), (2, 3), (0, 3), (0, 4), (0, 5), (1, 0),
        (1, 1), (1, 3), (1, 2), (1, 4), (1, 5), (2, 0), (2, 2), (2, 4), (2, 5),
    ]
    for k, m in order:
        w_copy(k, m).start()

    enc_pick = onehot_t(enc_send_ref[...], grid_rows)
    grid_copy.wait()
    picked = dot_t(enc_pick, grid_ref[...]).astype(BF)
    w_copy(0, 0).wait()
    enc_out[...] = dot(picked, w_ref[0, 0]).astype(BF)

    pl.semaphore_wait(barrier, n - 1)

    def halo(slot, src, dst_ref, target):
        return pltpu.make_async_remote_copy(
            src_ref=src,
            dst_ref=dst_ref,
            send_sem=halo_send.at[slot],
            recv_sem=halo_recv.at[slot],
            device_id=(part, target),
            device_id_type=MESH_ID,
        )

    def pair(slot, out_ref, table, cap, below_at, above_at):
        down = halo(slot, out_ref.at[pl.ds(0, cap), :], table.at[pl.ds(above_at, cap), :], jnp.maximum(me - 1, 0))
        up = halo(slot + 1, out_ref.at[pl.ds(cap, cap), :], table.at[pl.ds(below_at, cap), :], jnp.minimum(me + 1, n - 1))

        def start():
            @pl.when(has_below)
            def _():
                down.start()

            @pl.when(has_above)
            def _():
                up.start()

        def wait():
            @pl.when(has_above)
            def _():
                down.wait_recv()

            @pl.when(has_below)
            def _():
                up.wait_recv()

        def wait_send():
            @pl.when(has_below)
            def _():
                down.wait_send()

            @pl.when(has_above)
            def _():
                up.wait_send()

        return start, wait, wait_send

    enc_start, enc_wait, enc_done = pair(0, enc_out, enc_table, cap_g, 0, cap_g + grid_rows)
    enc_start()

    enc_table[pl.ds(cap_g, grid_rows), :] = dot(grid_ref[...], w_ref[0, 0]).astype(BF)
    w_copy(0, 1).wait()
    mesh_nodes = mesh_ref[...]
    live = lax.broadcasted_iota(jnp.int32, (1, enc_edges), 1) < enc_count_ref[0]
    enc_dst_t = onehot_t(jnp.where(live, enc_dst_ref[...], -1), mesh_rows)
    table_rows = 2 * cap_g + grid_rows
    tail = 128 - mesh_rows
    enc_table[pl.ds(table_rows, mesh_rows), :] = dot(mesh_nodes, w_ref[0, 1]).astype(BF)
    enc_table[pl.ds(table_rows + mesh_rows, tail), :] = raw_table(raww_ref[0], tail)
    enc_src = enc_src_ref[...]
    enc_src_t = onehot_t(enc_src, table_rows)
    enc_local_t = jnp.concatenate(
        [enc_src_t[cap_g : cap_g + grid_rows], enc_dst_t, raw_rows(enc_raw_ref[...], tail)], axis=0
    )
    enc_pre[...] = dot_t(
        enc_local_t,
        jnp.concatenate(
            [enc_table[pl.ds(cap_g, grid_rows), :], enc_table[pl.ds(table_rows, 128), :]], axis=0
        ),
    )
    w_copy(2, 1).wait()
    grid_dst[...] = dot(grid_ref[...], w_ref[2, 1])
    w_copy(2, 3).wait()
    grid_self[...] = dot(grid_ref[...], w_ref[2, 3])

    w_copy(0, 3).wait()
    mesh_self = dot(mesh_nodes, w_ref[0, 3])
    enc_wait()
    w_copy(0, 2).wait()
    enc_agg = jnp.zeros((mesh_rows, width), F32)
    step = 256
    for i in range(0, enc_edges, step):
        pre = (
            enc_pre[pl.ds(i, step), :]
            + dot_t(enc_src_t[:cap_g, i : i + step], enc_table[pl.ds(0, cap_g), :])
            + dot_t(enc_src_t[cap_g + grid_rows :, i : i + step], enc_table[pl.ds(cap_g + grid_rows, cap_g), :])
        )
        message = layer_norm(dot(silu(pre), w_ref[0, 2])).astype(BF)
        enc_agg = enc_agg + dot(enc_dst_t[:, i : i + step], message)

    w_copy(0, 4).wait()
    w_copy(0, 5).wait()
    hidden = silu(mesh_self + dot(enc_agg.astype(BF), w_ref[0, 4]))
    mesh_one_f = mesh_nodes.astype(F32) + layer_norm(dot(hidden, w_ref[0, 5]))
    mesh_one = mesh_one_f.astype(BF)

    w_copy(1, 0).wait()
    mesh_proj = dot(mesh_one, w_ref[1, 0]).astype(BF)
    lane = lax.broadcasted_iota(jnp.int32, (n, mesh_rows), 1)
    offers = proc_send_ref[0]
    for s in range(2):
        rows = dot((offers[:, s : s + 1] == lane).astype(F32).astype(BF), mesh_proj)
        for c in range(width // 128):
            far_out[pl.ds(s * 4 + c, n, stride=8), :] = rows[:, c * 128 : (c + 1) * 128]
    below_row = proc_send_ref[0, pl.ds(jnp.maximum(me - 1, 0), 1), :]
    above_row = proc_send_ref[0, pl.ds(jnp.minimum(me + 1, n - 1), 1), :]
    near_t = jnp.concatenate([onehot_t(below_row, mesh_rows), onehot_t(above_row, mesh_rows)], axis=1)
    proc_near_out[...] = dot_t(near_t, mesh_proj).astype(BF)

    proc_start, proc_wait, proc_done = pair(2, proc_near_out, proc_table, near, mesh_rows, mesh_rows + near)

    def far_copy(d, source, target):
        return pltpu.make_async_remote_copy(
            src_ref=far_out.at[pl.ds(pl.multiple_of(target * 8, 8), 8), :],
            dst_ref=far_in.at[pl.ds(pl.multiple_of(source * 8, 8), 8), :],
            send_sem=far_send_sem.at[d],
            recv_sem=far_recv_sem.at[d],
            device_id=(part, target),
            device_id_type=MESH_ID,
        )

    def far_start(d, carry):
        far_copy(d, me, lax.rem(me + d, n)).start()
        return carry

    proc_start()
    lax.fori_loop(1, n, far_start, 0)

    w_copy(1, 1).wait()
    w_copy(1, 3).wait()
    far_at = mesh_rows + 2 * near
    proc_table[pl.ds(0, mesh_rows), :] = mesh_proj
    proc_table[pl.ds(far_rows, mesh_rows), :] = dot(mesh_one, w_ref[1, 1]).astype(BF)
    proc_table[pl.ds(far_rows + mesh_rows, tail), :] = raw_table(raww_ref[1], tail)
    mesh_self = dot(mesh_one, w_ref[1, 3])
    live = lax.broadcasted_iota(jnp.int32, (1, proc_edges), 1) < proc_count_ref[0]
    proc_dst_t = onehot_t(jnp.where(live, proc_dst_ref[...], -1), mesh_rows)
    index = proc_src_ref[...]
    k = jnp.maximum(index - mesh_rows, 0)
    peer = lax.shift_right_logical(k, near.bit_length() - 1)
    slot = jnp.bitwise_and(k, near - 1)
    index = jnp.where(
        index < mesh_rows,
        index,
        jnp.where(
            peer == me - 1,
            mesh_rows + slot,
            jnp.where(peer == me + 1, mesh_rows + near + slot, far_at + slot * n + peer),
        ),
    )
    proc_all_t = jnp.concatenate(
        [onehot_t(index, far_rows), proc_dst_t, raw_rows(proc_raw_ref[...], tail)], axis=0
    )

    blocks = grid_rows // 128
    raw_high, raw_low = split(dec_raw_ref[...])
    stacked = []
    for q in range(blocks):
        cut = slice(q * 384, (q + 1) * 384)
        stacked += [
            dec_src_ref[:, cut].astype(F32),
            raw_high[:, cut].astype(F32),
            raw_low[:, cut].astype(F32),
            jnp.zeros((7, 384), F32),
        ]
    given = lax.broadcasted_iota(jnp.int32, (384, 384), 0)
    wanted = lax.broadcasted_iota(jnp.int32, (384, 384), 1)
    third = wanted // 128
    order_by_slot = (given == 3 * (wanted - 128 * third) + third).astype(F32).astype(BF)
    apart = dot(jnp.concatenate(stacked, axis=0).astype(BF), order_by_slot)
    dec_rows = mesh_rows + 2 * cap_d
    dec_table[pl.ds(dec_rows, 128 - dec_rows), :] = raw_table(raww_ref[2], 128 - dec_rows)

    proc_wait()

    def far_arrive(d, carry):
        far_copy(d, lax.rem(me + n - d, n), me).wait_recv()
        return carry

    lax.fori_loop(1, n, far_arrive, 0)
    for s in range(2):
        rows = [far_in[pl.ds(s * 4 + c, n, stride=8), :] for c in range(width // 128)]
        proc_table[pl.ds(far_at + s * n, n), :] = jnp.concatenate(rows, axis=1).astype(BF)

    w_copy(1, 2).wait()
    proc_agg = jnp.zeros((mesh_rows, width), F32)
    for i in range(0, proc_edges, step):
        pre = dot_t(proc_all_t[:, i : i + step], proc_table[...])
        message = layer_norm(dot(silu(pre), w_ref[1, 2])).astype(BF)
        proc_agg = proc_agg + dot(proc_dst_t[:, i : i + step], message)
    w_copy(1, 4).wait()
    w_copy(1, 5).wait()
    hidden = silu(mesh_self + dot(proc_agg.astype(BF), w_ref[1, 4]))
    mesh_out = (mesh_one.astype(F32) + layer_norm(dot(hidden, w_ref[1, 5]))).astype(BF)
    mesh_out_ref[...] = mesh_out

    w_copy(2, 0).wait()
    dec_proj = dot(mesh_out, w_ref[2, 0]).astype(BF)
    dec_table[pl.ds(cap_d, mesh_rows), :] = dec_proj
    dec_near_out[...] = dot_t(onehot_t(dec_send_ref[...], mesh_rows), dec_proj).astype(BF)
    dec_start, dec_wait, dec_done = pair(4, dec_near_out, dec_table, cap_d, 0, cap_d + mesh_rows)
    dec_start()
    w_copy(2, 2).wait()
    w_copy(2, 4).wait()
    w_copy(2, 5).wait()
    dec_wait()

    row_id = lax.broadcasted_iota(jnp.int32, (dec_rows, 128), 0).astype(F32)
    rest = jnp.zeros((128 - dec_rows - 12, 128), F32)
    out_copies = []
    for i in range(0, grid_rows, step):
        dec_agg = jnp.zeros((step, width), F32)
        for t in range(3):
            pieces = []
            for q in range(i // 128, (i + step) // 128):
                info = apart[q * 16 : (q + 1) * 16, t * 128 : (t + 1) * 128]
                high, low = info[1:5], info[5:9]
                pieces.append(
                    jnp.concatenate(
                        [(row_id == info[0:1]).astype(F32), high, low, high, rest], axis=0
                    ).astype(BF)
                )
            pre = dot_t(jnp.concatenate(pieces, axis=1), dec_table[...]) + grid_dst[pl.ds(i, step), :]
            message = layer_norm(dot(silu(pre), w_ref[2, 2])).astype(BF)
            dec_agg = dec_agg + message.astype(F32)
        hidden = silu(grid_self[pl.ds(i, step), :] + dot(dec_agg.astype(BF), w_ref[2, 4]))
        out_buf[pl.ds(i, step), :] = (
            grid_ref[pl.ds(i, step), :].astype(F32) + layer_norm(dot(hidden, w_ref[2, 5]))
        ).astype(BF)
        copy = pltpu.make_async_copy(
            out_buf.at[pl.ds(i, step), :], grid_out_hbm.at[pl.ds(i, step), :], out_sem.at[i // step]
        )
        copy.start()
        out_copies.append(copy)

    enc_done()
    proc_done()
    dec_done()

    def far_sent(d, carry):
        far_copy(d, me, lax.rem(me + d, n)).wait_send()
        return carry

    lax.fori_loop(1, n, far_sent, 0)
    for copy in out_copies:
        copy.wait()


def shards(
    grid_nodes,
    mesh_nodes,
    weights,
    raw_weights,
    enc_raw,
    enc_src,
    enc_dst,
    enc_count,
    enc_send,
    proc_raw,
    proc_src,
    proc_dst,
    proc_count,
    proc_send,
    dec_raw,
    dec_src,
    dec_send,
):
    n = lax.axis_size("band")
    grid_rows, width = grid_nodes.shape
    mesh_rows = mesh_nodes.shape[0]
    cap_g = enc_send.shape[1] // 2
    cap_d = dec_send.shape[1] // 2
    near = proc_send.shape[2]
    far_rows = -(-(mesh_rows + 2 * near + 2 * n) // 128) * 128
    vmem = pl.BlockSpec(memory_space=pltpu.VMEM)
    smem = pl.BlockSpec(memory_space=pltpu.SMEM)
    hbm = pl.BlockSpec(memory_space=pl.ANY)
    return pl.pallas_call(
        functools.partial(kernel, n, far_rows),
        out_shape=(
            jax.ShapeDtypeStruct(grid_nodes.shape, BF),
            jax.ShapeDtypeStruct(mesh_nodes.shape, BF),
        ),
        in_specs=[
            hbm, vmem, hbm, vmem,
            vmem, vmem, vmem, smem, vmem,
            vmem, vmem, vmem, smem, vmem,
            vmem, vmem, vmem,
        ],
        out_specs=(hbm, vmem),
        scratch_shapes=[
            pltpu.VMEM((grid_rows, width), BF),
            pltpu.VMEM(weights.shape, BF),
            pltpu.VMEM((2 * cap_g + grid_rows + 128, width), BF),
            pltpu.VMEM((2 * cap_g, width), BF),
            pltpu.VMEM((enc_src.shape[0], width), F32),
            pltpu.VMEM((far_rows + 128, width), BF),
            pltpu.VMEM((2 * near, width), BF),
            pltpu.VMEM((8 * n, 128), F32),
            pltpu.VMEM((8 * n, 128), F32),
            pltpu.VMEM((128, width), BF),
            pltpu.VMEM((2 * cap_d, width), BF),
            pltpu.VMEM((grid_rows, width), F32),
            pltpu.VMEM((grid_rows, width), F32),
            pltpu.VMEM((grid_rows, width), BF),
            pltpu.SemaphoreType.DMA(weights.shape[:2]),
            pltpu.SemaphoreType.DMA,
            pltpu.SemaphoreType.DMA((grid_rows // 256,)),
            pltpu.SemaphoreType.DMA((6,)),
            pltpu.SemaphoreType.DMA((6,)),
            pltpu.SemaphoreType.DMA((n,)),
            pltpu.SemaphoreType.DMA((n,)),
        ],
        compiler_params=pltpu.CompilerParams(
            collective_id=0, has_side_effects=True, vmem_limit_bytes=56 * 2**20
        ),
    )(
        grid_nodes, mesh_nodes, weights, raw_weights,
        enc_raw, enc_src[None, :], enc_dst[None, :], enc_count, enc_send,
        proc_raw, proc_src[None, :], proc_dst[None, :], proc_count, proc_send,
        dec_raw, dec_src[None, :], dec_send,
    )


def solution(mesh):
    placed = (
        P(("parts", "band"), None),
        P(("parts", "band"), None),
        P(),
        P(),
        P(None, "band"),
        P("band"),
        P("band"),
        P("band"),
        P("band", None),
        P(None, "band"),
        P("band"),
        P("band"),
        P("band"),
        P("band", None, None),
        P(None, "band"),
        P("band"),
        P("band", None),
    )
    return jax.shard_map(
        shards,
        mesh=mesh,
        in_specs=placed,
        out_specs=(P(("parts", "band"), None), P(("parts", "band"), None)),
        check_vma=False,
    )
```

```python
import functools

import jax
import jax.numpy as jnp
from jax import lax
from jax.experimental import pallas as pl
from jax.experimental.pallas import tpu as pltpu
from jax.sharding import PartitionSpec as P

BF = jnp.bfloat16
F32 = jnp.float32
MESH_ID = pl.DeviceIdType.MESH


def dot(a, b):
    return jnp.dot(a, b, preferred_element_type=F32)


def dot_t(a, b):
    return lax.dot_general(a, b, (((0,), (0,)), ((), ())), preferred_element_type=F32)


def silu(x):
    half = 0.5 * x
    return (half + half * jnp.tanh(half)).astype(BF)


def layer_norm(values):
    average = jnp.mean(values, axis=-1, keepdims=True)
    centred = values - average
    return centred * lax.rsqrt(jnp.mean(centred * centred, axis=-1, keepdims=True) + 1e-05)


def onehot_t(index_row, rows):
    lanes = index_row.shape[1]
    return (lax.broadcasted_iota(jnp.int32, (rows, lanes), 0) == index_row).astype(F32).astype(BF)


def row(ref):
    return ref[...].reshape(1, ref.shape[0])


def split(x):
    high = x.astype(BF)
    return high, (x - high.astype(F32)).astype(BF)


def raw_rows(raw, pad):
    high, low = split(raw)
    rest = jnp.zeros((pad - 3 * raw.shape[0], raw.shape[1]), F32)
    return jnp.concatenate([high.astype(F32), low.astype(F32), high.astype(F32), rest], axis=0).astype(BF)


def raw_table(raw_w, pad):
    high, low = split(raw_w)
    rest = jnp.zeros((pad - 3 * raw_w.shape[0], raw_w.shape[1]), F32)
    return jnp.concatenate([high.astype(F32), high.astype(F32), low.astype(F32), rest], axis=0).astype(BF)


def exchange_kernel(
    n,
    far_rows,
    grid_hbm,
    mesh_ref,
    w_hbm,
    raww_ref,
    enc_raw_ref,
    enc_src_ref,
    enc_dst_ref,
    enc_count_ref,
    enc_send_ref,
    proc_raw_ref,
    proc_src_ref,
    proc_dst_ref,
    proc_count_ref,
    proc_send_ref,
    dec_raw_ref,
    dec_src_ref,
    dec_send_ref,
    dec_table_hbm,
    apart_hbm,
    grid_dst_hbm,
    grid_self_hbm,
    mesh_out_hbm,
    grid_ref,
    w_ref,
    enc_table,
    enc_out,
    enc_pre,
    proc_table,
    proc_near_out,
    far_out,
    far_in,
    dec_table,
    dec_near_out,
    apart,
    grid_dst,
    grid_self,
    mesh_out_ref,
    w_sem,
    grid_sem,
    out_sem,
    halo_send,
    halo_recv,
    far_send_sem,
    far_recv_sem,
):
    me = lax.axis_index("band")
    part = lax.axis_index("parts")
    grid_rows = grid_ref.shape[0]
    width = grid_ref.shape[1]
    mesh_rows = mesh_ref.shape[0]
    enc_edges = enc_src_ref.shape[0]
    proc_edges = proc_src_ref.shape[0]
    cap_g = enc_send_ref.shape[1] // 2
    cap_d = dec_send_ref.shape[1] // 2
    near = proc_send_ref.shape[2]
    has_below = me > 0
    has_above = me < n - 1

    grid_copy = pltpu.make_async_copy(grid_hbm, grid_ref, grid_sem)
    grid_copy.start()

    def w_copy(k, m):
        return pltpu.make_async_copy(w_hbm.at[k, m], w_ref.at[k, m], w_sem.at[k, m])

    w_copy(0, 0).start()

    enc_table[pl.ds(0, cap_g), :] = jnp.zeros((cap_g, width), BF)
    enc_table[pl.ds(cap_g + grid_rows, cap_g), :] = jnp.zeros((cap_g, width), BF)
    proc_table[...] = jnp.zeros(proc_table.shape, BF)
    far_in[...] = jnp.zeros(far_in.shape, F32)
    dec_table[...] = jnp.zeros(dec_table.shape, BF)

    barrier = pltpu.get_barrier_semaphore()

    def greet(d, carry):
        pl.semaphore_signal(
            barrier, inc=1, device_id=(part, lax.rem(me + d, n)), device_id_type=MESH_ID
        )
        return carry

    lax.fori_loop(1, n, greet, 0)

    order = [
        (0, 1), (0, 2), (2, 1), (2, 3), (0, 3), (0, 4), (0, 5), (1, 0),
        (1, 1), (1, 3), (1, 2), (1, 4), (1, 5), (2, 0),
    ]
    for k, m in order:
        w_copy(k, m).start()

    enc_pick = onehot_t(enc_send_ref[...], grid_rows)
    grid_copy.wait()
    picked = dot_t(enc_pick, grid_ref[...]).astype(BF)
    w_copy(0, 0).wait()
    enc_out[...] = dot(picked, w_ref[0, 0]).astype(BF)

    pl.semaphore_wait(barrier, n - 1)

    def halo(slot, src, dst_ref, target):
        return pltpu.make_async_remote_copy(
            src_ref=src,
            dst_ref=dst_ref,
            send_sem=halo_send.at[slot],
            recv_sem=halo_recv.at[slot],
            device_id=(part, target),
            device_id_type=MESH_ID,
        )

    def pair(slot, out_ref, table, cap, below_at, above_at):
        down = halo(slot, out_ref.at[pl.ds(0, cap), :], table.at[pl.ds(above_at, cap), :], jnp.maximum(me - 1, 0))
        up = halo(slot + 1, out_ref.at[pl.ds(cap, cap), :], table.at[pl.ds(below_at, cap), :], jnp.minimum(me + 1, n - 1))

        def start():
            @pl.when(has_below)
            def _():
                down.start()

            @pl.when(has_above)
            def _():
                up.start()

        def wait():
            @pl.when(has_above)
            def _():
                down.wait_recv()

            @pl.when(has_below)
            def _():
                up.wait_recv()

        def wait_send():
            @pl.when(has_below)
            def _():
                down.wait_send()

            @pl.when(has_above)
            def _():
                up.wait_send()

        return start, wait, wait_send

    enc_start, enc_wait, enc_done = pair(0, enc_out, enc_table, cap_g, 0, cap_g + grid_rows)
    enc_start()

    enc_table[pl.ds(cap_g, grid_rows), :] = dot(grid_ref[...], w_ref[0, 0]).astype(BF)
    w_copy(0, 1).wait()
    mesh_nodes = mesh_ref[...]
    live = lax.broadcasted_iota(jnp.int32, (1, enc_edges), 1) < row(enc_count_ref)
    enc_dst_t = onehot_t(jnp.where(live, row(enc_dst_ref), -1), mesh_rows)
    table_rows = 2 * cap_g + grid_rows
    tail = 128 - mesh_rows
    enc_table[pl.ds(table_rows, mesh_rows), :] = dot(mesh_nodes, w_ref[0, 1]).astype(BF)
    enc_table[pl.ds(table_rows + mesh_rows, tail), :] = raw_table(raww_ref[0], tail)
    enc_src = row(enc_src_ref)
    enc_src_t = onehot_t(enc_src, table_rows)
    enc_local_t = jnp.concatenate(
        [enc_src_t[cap_g : cap_g + grid_rows], enc_dst_t, raw_rows(enc_raw_ref[...], tail)], axis=0
    )
    enc_pre[...] = dot_t(
        enc_local_t,
        jnp.concatenate(
            [enc_table[pl.ds(cap_g, grid_rows), :], enc_table[pl.ds(table_rows, 128), :]], axis=0
        ),
    )
    w_copy(2, 1).wait()
    grid_dst[...] = dot(grid_ref[...], w_ref[2, 1]).astype(BF)
    w_copy(2, 3).wait()
    grid_self[...] = dot(grid_ref[...], w_ref[2, 3]).astype(BF)

    def out_copy(src, dst, slot):
        return pltpu.make_async_copy(src, dst, out_sem.at[slot])

    dst_copy = out_copy(grid_dst, grid_dst_hbm, 0)
    dst_copy.start()
    self_copy = out_copy(grid_self, grid_self_hbm, 1)
    self_copy.start()

    w_copy(0, 3).wait()
    mesh_self = dot(mesh_nodes, w_ref[0, 3])
    enc_wait()
    w_copy(0, 2).wait()
    enc_agg = jnp.zeros((mesh_rows, width), F32)
    step = 256
    for i in range(0, enc_edges, step):
        pre = (
            enc_pre[pl.ds(i, step), :]
            + dot_t(enc_src_t[:cap_g, i : i + step], enc_table[pl.ds(0, cap_g), :])
            + dot_t(enc_src_t[cap_g + grid_rows :, i : i + step], enc_table[pl.ds(cap_g + grid_rows, cap_g), :])
        )
        message = layer_norm(dot(silu(pre), w_ref[0, 2])).astype(BF)
        enc_agg = enc_agg + dot(enc_dst_t[:, i : i + step], message)

    w_copy(0, 4).wait()
    w_copy(0, 5).wait()
    hidden = silu(mesh_self + dot(enc_agg.astype(BF), w_ref[0, 4]))
    mesh_one_f = mesh_nodes.astype(F32) + layer_norm(dot(hidden, w_ref[0, 5]))
    mesh_one = mesh_one_f.astype(BF)

    w_copy(1, 0).wait()
    mesh_proj = dot(mesh_one, w_ref[1, 0]).astype(BF)
    lane = lax.broadcasted_iota(jnp.int32, (n, mesh_rows), 1)
    offers = proc_send_ref[0]
    for s in range(2):
        rows = dot((offers[:, s : s + 1] == lane).astype(F32).astype(BF), mesh_proj)
        for c in range(width // 128):
            far_out[pl.ds(s * 4 + c, n, stride=8), :] = rows[:, c * 128 : (c + 1) * 128]
    below_row = proc_send_ref[0, pl.ds(jnp.maximum(me - 1, 0), 1), :]
    above_row = proc_send_ref[0, pl.ds(jnp.minimum(me + 1, n - 1), 1), :]
    near_t = jnp.concatenate([onehot_t(below_row, mesh_rows), onehot_t(above_row, mesh_rows)], axis=1)
    proc_near_out[...] = dot_t(near_t, mesh_proj).astype(BF)

    proc_start, proc_wait, proc_done = pair(2, proc_near_out, proc_table, near, mesh_rows, mesh_rows + near)

    def far_copy(d, source, target):
        return pltpu.make_async_remote_copy(
            src_ref=far_out.at[pl.ds(pl.multiple_of(target * 8, 8), 8), :],
            dst_ref=far_in.at[pl.ds(pl.multiple_of(source * 8, 8), 8), :],
            send_sem=far_send_sem.at[d],
            recv_sem=far_recv_sem.at[d],
            device_id=(part, target),
            device_id_type=MESH_ID,
        )

    def far_start(d, carry):
        far_copy(d, me, lax.rem(me + d, n)).start()
        return carry

    proc_start()
    lax.fori_loop(1, n, far_start, 0)

    w_copy(1, 1).wait()
    w_copy(1, 3).wait()
    far_at = mesh_rows + 2 * near
    proc_table[pl.ds(0, mesh_rows), :] = mesh_proj
    proc_table[pl.ds(far_rows, mesh_rows), :] = dot(mesh_one, w_ref[1, 1]).astype(BF)
    proc_table[pl.ds(far_rows + mesh_rows, tail), :] = raw_table(raww_ref[1], tail)
    mesh_self = dot(mesh_one, w_ref[1, 3])
    live = lax.broadcasted_iota(jnp.int32, (1, proc_edges), 1) < row(proc_count_ref)
    proc_dst_t = onehot_t(jnp.where(live, row(proc_dst_ref), -1), mesh_rows)
    index = row(proc_src_ref)
    k = jnp.maximum(index - mesh_rows, 0)
    peer = lax.shift_right_logical(k, near.bit_length() - 1)
    slot = jnp.bitwise_and(k, near - 1)
    index = jnp.where(
        index < mesh_rows,
        index,
        jnp.where(
            peer == me - 1,
            mesh_rows + slot,
            jnp.where(peer == me + 1, mesh_rows + near + slot, far_at + slot * n + peer),
        ),
    )
    proc_all_t = jnp.concatenate(
        [onehot_t(index, far_rows), proc_dst_t, raw_rows(proc_raw_ref[...], tail)], axis=0
    )

    blocks = grid_rows // 128
    raw_high, raw_low = split(dec_raw_ref[...])
    stacked = []
    dec_src = row(dec_src_ref).astype(F32)
    for q in range(blocks):
        cut = slice(q * 384, (q + 1) * 384)
        stacked += [
            dec_src[:, cut],
            raw_high[:, cut].astype(F32),
            raw_low[:, cut].astype(F32),
            jnp.zeros((7, 384), F32),
        ]
    given = lax.broadcasted_iota(jnp.int32, (384, 384), 0)
    wanted = lax.broadcasted_iota(jnp.int32, (384, 384), 1)
    third = wanted // 128
    order_by_slot = (given == 3 * (wanted - 128 * third) + third).astype(F32).astype(BF)
    apart[...] = dot(jnp.concatenate(stacked, axis=0).astype(BF), order_by_slot)
    apart_copy = out_copy(apart, apart_hbm, 2)
    apart_copy.start()
    dec_rows = mesh_rows + 2 * cap_d
    dec_table[pl.ds(dec_rows, 128 - dec_rows), :] = raw_table(raww_ref[2], 128 - dec_rows)

    proc_wait()

    def far_arrive(d, carry):
        far_copy(d, lax.rem(me + n - d, n), me).wait_recv()
        return carry

    lax.fori_loop(1, n, far_arrive, 0)
    for s in range(2):
        rows = [far_in[pl.ds(s * 4 + c, n, stride=8), :] for c in range(width // 128)]
        proc_table[pl.ds(far_at + s * n, n), :] = jnp.concatenate(rows, axis=1).astype(BF)

    w_copy(1, 2).wait()
    proc_agg = jnp.zeros((mesh_rows, width), F32)
    for i in range(0, proc_edges, step):
        pre = dot_t(proc_all_t[:, i : i + step], proc_table[...])
        message = layer_norm(dot(silu(pre), w_ref[1, 2])).astype(BF)
        proc_agg = proc_agg + dot(proc_dst_t[:, i : i + step], message)
    w_copy(1, 4).wait()
    w_copy(1, 5).wait()
    hidden = silu(mesh_self + dot(proc_agg.astype(BF), w_ref[1, 4]))
    mesh_out = (mesh_one.astype(F32) + layer_norm(dot(hidden, w_ref[1, 5]))).astype(BF)
    mesh_out_ref[...] = mesh_out
    mesh_copy = out_copy(mesh_out_ref, mesh_out_hbm, 3)
    mesh_copy.start()

    w_copy(2, 0).wait()
    dec_proj = dot(mesh_out, w_ref[2, 0]).astype(BF)
    dec_table[pl.ds(cap_d, mesh_rows), :] = dec_proj
    dec_near_out[...] = dot_t(onehot_t(dec_send_ref[...], mesh_rows), dec_proj).astype(BF)
    dec_start, dec_wait, dec_done = pair(4, dec_near_out, dec_table_hbm, cap_d, 0, cap_d + mesh_rows)
    dec_start()
    own = pl.ds(cap_d, mesh_rows)
    own_copy = out_copy(dec_table.at[own, :], dec_table_hbm.at[own, :], 4)
    own_copy.start()
    raw_at = pl.ds(dec_rows, 128 - dec_rows)
    raw_copy = out_copy(dec_table.at[raw_at, :], dec_table_hbm.at[raw_at, :], 5)
    raw_copy.start()
    rim = pl.ds(jnp.where(has_below, cap_d + mesh_rows, 0), cap_d)
    rim_copy = out_copy(dec_table.at[pl.ds(0, cap_d), :], dec_table_hbm.at[rim, :], 6)

    @pl.when(jnp.logical_not(jnp.logical_and(has_below, has_above)))
    def _():
        rim_copy.start()
        rim_copy.wait()

    dec_wait()

    enc_done()
    proc_done()
    dec_done()

    def far_sent(d, carry):
        far_copy(d, me, lax.rem(me + d, n)).wait_send()
        return carry

    lax.fori_loop(1, n, far_sent, 0)
    for copy in (dst_copy, self_copy, apart_copy, mesh_copy, own_copy, raw_copy):
        copy.wait()


def decode_kernel(
    dec_rows,
    grid_hbm,
    w_hbm,
    dec_table_hbm,
    apart_hbm,
    grid_dst_hbm,
    grid_self_hbm,
    mesh_hbm,
    grid_out_hbm,
    mesh_out_hbm,
    grid_ref,
    w_ref,
    dec_table,
    apart,
    grid_dst,
    grid_self,
    out_buf,
    in_sem,
    out_sem,
):
    grid_rows, width = grid_ref.shape
    step = 256
    loads = [
        pltpu.make_async_copy(src, dst, in_sem.at[i])
        for i, (src, dst) in enumerate(
            [
                (dec_table_hbm, dec_table),
                (apart_hbm, apart),
                (grid_dst_hbm, grid_dst),
                (w_hbm.at[2, 2], w_ref.at[0]),
                (w_hbm.at[2, 4], w_ref.at[1]),
                (grid_self_hbm, grid_self),
                (w_hbm.at[2, 5], w_ref.at[2]),
                (grid_hbm, grid_ref),
                (mesh_hbm, mesh_out_hbm),
            ]
        )
    ]
    for load in loads:
        load.start()
    for load in loads[:4]:
        load.wait()
    row_id = lax.broadcasted_iota(jnp.int32, (dec_rows, 128), 0).astype(F32)
    rest = jnp.zeros((128 - dec_rows - 12, 128), F32)
    out_copies = []
    for i in range(0, grid_rows, step):
        dec_agg = jnp.zeros((step, width), F32)
        for t in range(3):
            pieces = []
            for q in range(i // 128, (i + step) // 128):
                info = apart[q * 16 : (q + 1) * 16, t * 128 : (t + 1) * 128]
                high, low = info[1:5], info[5:9]
                pieces.append(
                    jnp.concatenate(
                        [(row_id == info[0:1]).astype(F32), high, low, high, rest], axis=0
                    ).astype(BF)
                )
            pre = dot_t(jnp.concatenate(pieces, axis=1), dec_table[...]) + grid_dst[
                pl.ds(i, step), :
            ].astype(F32)
            message = layer_norm(dot(silu(pre), w_ref[0])).astype(BF)
            dec_agg = dec_agg + message.astype(F32)
        if i == 0:
            loads[4].wait()
            loads[5].wait()
        hidden = silu(grid_self[pl.ds(i, step), :].astype(F32) + dot(dec_agg.astype(BF), w_ref[1]))
        if i == 0:
            loads[6].wait()
            loads[7].wait()
        out_buf[pl.ds(i, step), :] = (
            grid_ref[pl.ds(i, step), :].astype(F32) + layer_norm(dot(hidden, w_ref[2]))
        ).astype(BF)
        copy = pltpu.make_async_copy(
            out_buf.at[pl.ds(i, step), :], grid_out_hbm.at[pl.ds(i, step), :], out_sem.at[i // step]
        )
        copy.start()
        out_copies.append(copy)
    loads[8].wait()
    for copy in out_copies:
        copy.wait()


def shards(
    grid_nodes,
    mesh_nodes,
    weights,
    raw_weights,
    enc_raw,
    enc_src,
    enc_dst,
    enc_count,
    enc_send,
    proc_raw,
    proc_src,
    proc_dst,
    proc_count,
    proc_send,
    dec_raw,
    dec_src,
    dec_send,
):
    n = lax.axis_size("band")
    grid_rows, width = grid_nodes.shape
    mesh_rows = mesh_nodes.shape[0]
    cap_g = enc_send.shape[1] // 2
    cap_d = dec_send.shape[1] // 2
    near = proc_send.shape[2]
    far_rows = -(-(mesh_rows + 2 * near + 2 * n) // 128) * 128
    vmem = pl.BlockSpec(memory_space=pltpu.VMEM)
    hbm = pl.BlockSpec(memory_space=pl.ANY)
    dec_table, apart, grid_dst, grid_self, mesh_out = pl.pallas_call(
        functools.partial(exchange_kernel, n, far_rows),
        out_shape=(
            jax.ShapeDtypeStruct((128, width), BF),
            jax.ShapeDtypeStruct((grid_rows // 8, 384), F32),
            jax.ShapeDtypeStruct(grid_nodes.shape, BF),
            jax.ShapeDtypeStruct(grid_nodes.shape, BF),
            jax.ShapeDtypeStruct(mesh_nodes.shape, BF),
        ),
        in_specs=[
            hbm, vmem, hbm, vmem,
            vmem, vmem, vmem, vmem, vmem,
            vmem, vmem, vmem, vmem, vmem,
            vmem, vmem, vmem,
        ],
        out_specs=(hbm,) * 5,
        scratch_shapes=[
            pltpu.VMEM((grid_rows, width), BF),
            pltpu.VMEM(weights.shape, BF),
            pltpu.VMEM((2 * cap_g + grid_rows + 128, width), BF),
            pltpu.VMEM((2 * cap_g, width), BF),
            pltpu.VMEM((enc_src.shape[0], width), F32),
            pltpu.VMEM((far_rows + 128, width), BF),
            pltpu.VMEM((2 * near, width), BF),
            pltpu.VMEM((8 * n, 128), F32),
            pltpu.VMEM((8 * n, 128), F32),
            pltpu.VMEM((128, width), BF),
            pltpu.VMEM((2 * cap_d, width), BF),
            pltpu.VMEM((grid_rows // 8, 384), F32),
            pltpu.VMEM((grid_rows, width), BF),
            pltpu.VMEM((grid_rows, width), BF),
            pltpu.VMEM(mesh_nodes.shape, BF),
            pltpu.SemaphoreType.DMA(weights.shape[:2]),
            pltpu.SemaphoreType.DMA,
            pltpu.SemaphoreType.DMA((7,)),
            pltpu.SemaphoreType.DMA((6,)),
            pltpu.SemaphoreType.DMA((6,)),
            pltpu.SemaphoreType.DMA((n,)),
            pltpu.SemaphoreType.DMA((n,)),
        ],
        compiler_params=pltpu.CompilerParams(
            collective_id=0, has_side_effects=True, vmem_limit_bytes=56 * 2**20
        ),
    )(
        grid_nodes, mesh_nodes, weights, raw_weights,
        enc_raw, enc_src, enc_dst, enc_count, enc_send,
        proc_raw, proc_src, proc_dst, proc_count, proc_send,
        dec_raw, dec_src, dec_send,
    )
    return pl.pallas_call(
        functools.partial(decode_kernel, mesh_rows + 2 * cap_d),
        out_shape=(
            jax.ShapeDtypeStruct(grid_nodes.shape, BF),
            jax.ShapeDtypeStruct(mesh_nodes.shape, BF),
        ),
        in_specs=[hbm] * 7,
        out_specs=(hbm, hbm),
        scratch_shapes=[
            pltpu.VMEM((grid_rows, width), BF),
            pltpu.VMEM((3, width, width), BF),
            pltpu.VMEM((128, width), BF),
            pltpu.VMEM((grid_rows // 8, 384), F32),
            pltpu.VMEM((grid_rows, width), BF),
            pltpu.VMEM((grid_rows, width), BF),
            pltpu.VMEM((grid_rows, width), BF),
            pltpu.SemaphoreType.DMA((9,)),
            pltpu.SemaphoreType.DMA((grid_rows // 256,)),
        ],
        compiler_params=pltpu.CompilerParams(vmem_limit_bytes=56 * 2**20),
    )(grid_nodes, weights, dec_table, apart, grid_dst, grid_self, mesh_out)


def solution(mesh):
    placed = (
        P(("parts", "band"), None),
        P(("parts", "band"), None),
        P(),
        P(),
        P(None, "band"),
        P("band"),
        P("band"),
        P("band"),
        P("band", None),
        P(None, "band"),
        P("band"),
        P("band"),
        P("band"),
        P("band", None, None),
        P(None, "band"),
        P("band"),
        P("band", None),
    )
    return jax.shard_map(
        shards,
        mesh=mesh,
        in_specs=placed,
        out_specs=(P(("parts", "band"), None), P(("parts", "band"), None)),
        check_vma=False,
    )
```

```python
import functools

import jax
import jax.numpy as jnp
from jax import lax
from jax.experimental import pallas as pl
from jax.experimental.pallas import tpu as pltpu
from jax.sharding import PartitionSpec as P

BF = jnp.bfloat16
F32 = jnp.float32
MESH_ID = pl.DeviceIdType.MESH


def dot(a, b):
    return jnp.dot(a, b, preferred_element_type=F32)


def dot_t(a, b):
    return lax.dot_general(a, b, (((0,), (0,)), ((), ())), preferred_element_type=F32)


def silu(x):
    half = 0.5 * x
    return (half + half * jnp.tanh(half)).astype(BF)


def layer_norm(values):
    average = jnp.mean(values, axis=-1, keepdims=True)
    centred = values - average
    return centred * lax.rsqrt(jnp.mean(centred * centred, axis=-1, keepdims=True) + 1e-05)


def onehot_t(index_row, rows):
    lanes = index_row.shape[1]
    return (lax.broadcasted_iota(jnp.int32, (rows, lanes), 0) == index_row).astype(F32).astype(BF)


def row(ref):
    return ref[...].reshape(1, ref.shape[0])


def split(x):
    high = x.astype(BF)
    return high, (x - high.astype(F32)).astype(BF)


def raw_rows(raw, pad):
    high, low = split(raw)
    rest = jnp.zeros((pad - 3 * raw.shape[0], raw.shape[1]), F32)
    return jnp.concatenate([high.astype(F32), low.astype(F32), high.astype(F32), rest], axis=0).astype(BF)


def raw_table(raw_w, pad):
    high, low = split(raw_w)
    rest = jnp.zeros((pad - 3 * raw_w.shape[0], raw_w.shape[1]), F32)
    return jnp.concatenate([high.astype(F32), high.astype(F32), low.astype(F32), rest], axis=0).astype(BF)


def exchange_kernel(
    n,
    far_rows,
    grid_hbm,
    mesh_in,
    w_hbm,
    raww_in,
    enc_raw_in,
    enc_src_in,
    enc_dst_in,
    enc_count_ref,
    enc_send_in,
    proc_raw_in,
    proc_src_in,
    proc_dst_in,
    proc_count_ref,
    proc_send_in,
    dec_raw_in,
    dec_src_in,
    dec_send_in,
    dec_table_hbm,
    apart_hbm,
    grid_dst_hbm,
    grid_self_hbm,
    mesh_out_hbm,
    grid_ref,
    w_ref,
    enc_table,
    enc_out,
    enc_pre,
    proc_table,
    proc_near_out,
    far_out,
    far_in,
    dec_table,
    dec_near_out,
    apart,
    grid_dst,
    grid_self,
    mesh_out_ref,
    w_sem,
    grid_sem,
    out_sem,
    halo_send,
    halo_recv,
    far_send_sem,
    far_recv_sem,
    mesh_ref,
    raww_ref,
    enc_raw_ref,
    enc_src_ref,
    enc_dst_ref,
    enc_send_ref,
    proc_raw_ref,
    proc_src_ref,
    proc_dst_ref,
    proc_send_ref,
    dec_raw_ref,
    dec_src_ref,
    dec_send_ref,
    small_sem,
):
    me = lax.axis_index("band")
    part = lax.axis_index("parts")
    grid_rows = grid_ref.shape[0]
    width = grid_ref.shape[1]
    mesh_rows = mesh_ref.shape[0]
    enc_edges = enc_src_ref.shape[0]
    proc_edges = proc_src_ref.shape[0]
    cap_g = enc_send_ref.shape[1] // 2
    cap_d = dec_send_ref.shape[1] // 2
    near = proc_send_ref.shape[2]
    has_below = me > 0
    has_above = me < n - 1

    grid_copy = pltpu.make_async_copy(grid_hbm, grid_ref, grid_sem)
    grid_copy.start()
    smalls = [
        (mesh_in, mesh_ref),
        (raww_in, raww_ref),
        (enc_raw_in, enc_raw_ref),
        (enc_src_in, enc_src_ref),
        (enc_dst_in, enc_dst_ref),
        (enc_send_in, enc_send_ref),
        (proc_raw_in, proc_raw_ref),
        (proc_src_in, proc_src_ref),
        (proc_dst_in, proc_dst_ref),
        (proc_send_in, proc_send_ref),
        (dec_raw_in, dec_raw_ref),
        (dec_src_in, dec_src_ref),
        (dec_send_in, dec_send_ref),
    ]
    small_copies = [
        pltpu.make_async_copy(src, dst, small_sem.at[i]) for i, (src, dst) in enumerate(smalls)
    ]
    small_copies[5].start()

    def w_copy(k, m):
        return pltpu.make_async_copy(w_hbm.at[k, m], w_ref.at[k, m], w_sem.at[k, m])

    w_copy(0, 0).start()
    for i, small in enumerate(small_copies):
        if i != 5:
            small.start()

    enc_table[pl.ds(0, cap_g), :] = jnp.zeros((cap_g, width), BF)
    enc_table[pl.ds(cap_g + grid_rows, cap_g), :] = jnp.zeros((cap_g, width), BF)
    proc_table[...] = jnp.zeros(proc_table.shape, BF)
    far_in[...] = jnp.zeros(far_in.shape, F32)
    dec_table[...] = jnp.zeros(dec_table.shape, BF)

    barrier = pltpu.get_barrier_semaphore()

    def greet(d, carry):
        pl.semaphore_signal(
            barrier, inc=1, device_id=(part, lax.rem(me + d, n)), device_id_type=MESH_ID
        )
        return carry

    lax.fori_loop(1, n, greet, 0)

    small_copies[5].wait()
    enc_pick = onehot_t(enc_send_ref[...], grid_rows)
    grid_copy.wait()
    picked = dot_t(enc_pick, grid_ref[...]).astype(BF)
    w_copy(0, 0).wait()
    order = [
        (0, 1), (2, 1), (0, 3), (0, 2), (0, 4), (0, 5), (1, 0),
        (1, 1), (1, 3), (2, 3), (1, 2), (1, 4), (1, 5), (2, 0),
    ]
    for k, m in order:
        w_copy(k, m).start()
    enc_out[...] = dot(picked, w_ref[0, 0]).astype(BF)
    for i, small in enumerate(small_copies):
        if i != 5:
            small.wait()

    pl.semaphore_wait(barrier, n - 1)

    def halo(slot, src, dst_ref, target):
        return pltpu.make_async_remote_copy(
            src_ref=src,
            dst_ref=dst_ref,
            send_sem=halo_send.at[slot],
            recv_sem=halo_recv.at[slot],
            device_id=(part, target),
            device_id_type=MESH_ID,
        )

    def pair(slot, out_ref, table, cap, below_at, above_at):
        down = halo(slot, out_ref.at[pl.ds(0, cap), :], table.at[pl.ds(above_at, cap), :], jnp.maximum(me - 1, 0))
        up = halo(slot + 1, out_ref.at[pl.ds(cap, cap), :], table.at[pl.ds(below_at, cap), :], jnp.minimum(me + 1, n - 1))

        def start():
            @pl.when(has_below)
            def _():
                down.start()

            @pl.when(has_above)
            def _():
                up.start()

        def wait():
            @pl.when(has_above)
            def _():
                down.wait_recv()

            @pl.when(has_below)
            def _():
                up.wait_recv()

        def wait_send():
            @pl.when(has_below)
            def _():
                down.wait_send()

            @pl.when(has_above)
            def _():
                up.wait_send()

        return start, wait, wait_send

    enc_start, enc_wait, enc_done = pair(0, enc_out, enc_table, cap_g, 0, cap_g + grid_rows)
    enc_start()

    enc_table[pl.ds(cap_g, grid_rows), :] = dot(grid_ref[...], w_ref[0, 0]).astype(BF)
    w_copy(0, 1).wait()
    mesh_nodes = mesh_ref[...]
    live = lax.broadcasted_iota(jnp.int32, (1, enc_edges), 1) < enc_count_ref[0]
    enc_dst_t = onehot_t(jnp.where(live, row(enc_dst_ref), -1), mesh_rows)
    table_rows = 2 * cap_g + grid_rows
    tail = 128 - mesh_rows
    enc_table[pl.ds(table_rows, mesh_rows), :] = dot(mesh_nodes, w_ref[0, 1]).astype(BF)
    enc_table[pl.ds(table_rows + mesh_rows, tail), :] = raw_table(raww_ref[0], tail)
    enc_src = row(enc_src_ref)
    enc_src_t = onehot_t(enc_src, table_rows)
    enc_local_t = jnp.concatenate(
        [enc_src_t[cap_g : cap_g + grid_rows], enc_dst_t, raw_rows(enc_raw_ref[...], tail)], axis=0
    )
    enc_pre[...] = dot_t(
        enc_local_t,
        jnp.concatenate(
            [enc_table[pl.ds(cap_g, grid_rows), :], enc_table[pl.ds(table_rows, 128), :]], axis=0
        ),
    )
    w_copy(2, 1).wait()
    grid_dst[...] = dot(grid_ref[...], w_ref[2, 1]).astype(BF)

    def out_copy(src, dst, slot):
        return pltpu.make_async_copy(src, dst, out_sem.at[slot])

    dst_copy = out_copy(grid_dst, grid_dst_hbm, 0)
    dst_copy.start()

    w_copy(0, 3).wait()
    mesh_self = dot(mesh_nodes, w_ref[0, 3])
    enc_wait()
    w_copy(0, 2).wait()
    enc_agg = jnp.zeros((mesh_rows, width), F32)
    step = 256
    for i in range(0, enc_edges, step):
        pre = (
            enc_pre[pl.ds(i, step), :]
            + dot_t(enc_src_t[:cap_g, i : i + step], enc_table[pl.ds(0, cap_g), :])
            + dot_t(enc_src_t[cap_g + grid_rows :, i : i + step], enc_table[pl.ds(cap_g + grid_rows, cap_g), :])
        )
        message = layer_norm(dot(silu(pre), w_ref[0, 2])).astype(BF)
        enc_agg = enc_agg + dot(enc_dst_t[:, i : i + step], message)

    w_copy(0, 4).wait()
    w_copy(0, 5).wait()
    hidden = silu(mesh_self + dot(enc_agg.astype(BF), w_ref[0, 4]))
    mesh_one_f = mesh_nodes.astype(F32) + layer_norm(dot(hidden, w_ref[0, 5]))
    mesh_one = mesh_one_f.astype(BF)

    w_copy(1, 0).wait()
    mesh_proj = dot(mesh_one, w_ref[1, 0]).astype(BF)
    lane = lax.broadcasted_iota(jnp.int32, (n, mesh_rows), 1)
    offers = proc_send_ref[0]
    for s in range(2):
        rows = dot((offers[:, s : s + 1] == lane).astype(F32).astype(BF), mesh_proj)
        for c in range(width // 128):
            far_out[pl.ds(s * 4 + c, n, stride=8), :] = rows[:, c * 128 : (c + 1) * 128]
    below_row = proc_send_ref[0, pl.ds(jnp.maximum(me - 1, 0), 1), :]
    above_row = proc_send_ref[0, pl.ds(jnp.minimum(me + 1, n - 1), 1), :]
    near_t = jnp.concatenate([onehot_t(below_row, mesh_rows), onehot_t(above_row, mesh_rows)], axis=1)
    proc_near_out[...] = dot_t(near_t, mesh_proj).astype(BF)

    proc_start, proc_wait, proc_done = pair(2, proc_near_out, proc_table, near, mesh_rows, mesh_rows + near)

    def far_copy(d, source, target):
        return pltpu.make_async_remote_copy(
            src_ref=far_out.at[pl.ds(pl.multiple_of(target * 8, 8), 8), :],
            dst_ref=far_in.at[pl.ds(pl.multiple_of(source * 8, 8), 8), :],
            send_sem=far_send_sem.at[d],
            recv_sem=far_recv_sem.at[d],
            device_id=(part, target),
            device_id_type=MESH_ID,
        )

    def far_start(d, carry):
        far_copy(d, me, lax.rem(me + d, n)).start()
        return carry

    proc_start()
    lax.fori_loop(1, n, far_start, 0)

    w_copy(1, 1).wait()
    w_copy(1, 3).wait()
    far_at = mesh_rows + 2 * near
    proc_table[pl.ds(0, mesh_rows), :] = mesh_proj
    proc_table[pl.ds(far_rows, mesh_rows), :] = dot(mesh_one, w_ref[1, 1]).astype(BF)
    proc_table[pl.ds(far_rows + mesh_rows, tail), :] = raw_table(raww_ref[1], tail)
    mesh_self = dot(mesh_one, w_ref[1, 3])
    live = lax.broadcasted_iota(jnp.int32, (1, proc_edges), 1) < proc_count_ref[0]
    proc_dst_t = onehot_t(jnp.where(live, row(proc_dst_ref), -1), mesh_rows)
    index = row(proc_src_ref)
    k = jnp.maximum(index - mesh_rows, 0)
    peer = lax.shift_right_logical(k, near.bit_length() - 1)
    slot = jnp.bitwise_and(k, near - 1)
    index = jnp.where(
        index < mesh_rows,
        index,
        jnp.where(
            peer == me - 1,
            mesh_rows + slot,
            jnp.where(peer == me + 1, mesh_rows + near + slot, far_at + slot * n + peer),
        ),
    )
    proc_all_t = jnp.concatenate(
        [onehot_t(index, far_rows), proc_dst_t, raw_rows(proc_raw_ref[...], tail)], axis=0
    )

    w_copy(2, 3).wait()
    grid_self[...] = dot(grid_ref[...], w_ref[2, 3]).astype(BF)
    self_copy = out_copy(grid_self, grid_self_hbm, 1)
    self_copy.start()

    proc_wait()

    def far_arrive(d, carry):
        far_copy(d, lax.rem(me + n - d, n), me).wait_recv()
        return carry

    lax.fori_loop(1, n, far_arrive, 0)
    for s in range(2):
        rows = [far_in[pl.ds(s * 4 + c, n, stride=8), :] for c in range(width // 128)]
        proc_table[pl.ds(far_at + s * n, n), :] = jnp.concatenate(rows, axis=1).astype(BF)

    w_copy(1, 2).wait()
    proc_agg = jnp.zeros((mesh_rows, width), F32)
    for i in range(0, proc_edges, step):
        pre = dot_t(proc_all_t[:, i : i + step], proc_table[...])
        message = layer_norm(dot(silu(pre), w_ref[1, 2])).astype(BF)
        proc_agg = proc_agg + dot(proc_dst_t[:, i : i + step], message)
    w_copy(1, 4).wait()
    w_copy(1, 5).wait()
    hidden = silu(mesh_self + dot(proc_agg.astype(BF), w_ref[1, 4]))
    mesh_out = (mesh_one.astype(F32) + layer_norm(dot(hidden, w_ref[1, 5]))).astype(BF)
    mesh_out_ref[...] = mesh_out
    mesh_copy = out_copy(mesh_out_ref, mesh_out_hbm, 3)
    mesh_copy.start()

    w_copy(2, 0).wait()
    dec_proj = dot(mesh_out, w_ref[2, 0]).astype(BF)
    dec_table[pl.ds(cap_d, mesh_rows), :] = dec_proj
    dec_near_out[...] = dot_t(onehot_t(dec_send_ref[...], mesh_rows), dec_proj).astype(BF)
    dec_start, dec_wait, dec_done = pair(4, dec_near_out, dec_table_hbm, cap_d, 0, cap_d + mesh_rows)
    dec_start()
    blocks = grid_rows // 128
    raw_high, raw_low = split(dec_raw_ref[...])
    stacked = []
    dec_src = row(dec_src_ref).astype(F32)
    for q in range(blocks):
        cut = slice(q * 384, (q + 1) * 384)
        stacked += [
            dec_src[:, cut],
            raw_high[:, cut].astype(F32),
            raw_low[:, cut].astype(F32),
            jnp.zeros((7, 384), F32),
        ]
    given = lax.broadcasted_iota(jnp.int32, (384, 384), 0)
    wanted = lax.broadcasted_iota(jnp.int32, (384, 384), 1)
    third = wanted // 128
    order_by_slot = (given == 3 * (wanted - 128 * third) + third).astype(F32).astype(BF)
    apart[...] = dot(jnp.concatenate(stacked, axis=0).astype(BF), order_by_slot)
    apart_copy = out_copy(apart, apart_hbm, 2)
    apart_copy.start()
    dec_rows = mesh_rows + 2 * cap_d
    dec_table[pl.ds(dec_rows, 128 - dec_rows), :] = raw_table(raww_ref[2], 128 - dec_rows)

    own = pl.ds(cap_d, mesh_rows)
    own_copy = out_copy(dec_table.at[own, :], dec_table_hbm.at[own, :], 4)
    own_copy.start()
    raw_at = pl.ds(dec_rows, 128 - dec_rows)
    raw_copy = out_copy(dec_table.at[raw_at, :], dec_table_hbm.at[raw_at, :], 5)
    raw_copy.start()
    rim = pl.ds(jnp.where(has_below, cap_d + mesh_rows, 0), cap_d)
    rim_copy = out_copy(dec_table.at[pl.ds(0, cap_d), :], dec_table_hbm.at[rim, :], 6)

    @pl.when(jnp.logical_not(jnp.logical_and(has_below, has_above)))
    def _():
        rim_copy.start()
        rim_copy.wait()

    dec_wait()

    enc_done()
    proc_done()
    dec_done()

    def far_sent(d, carry):
        far_copy(d, me, lax.rem(me + d, n)).wait_send()
        return carry

    lax.fori_loop(1, n, far_sent, 0)
    for copy in (dst_copy, self_copy, apart_copy, mesh_copy, own_copy, raw_copy):
        copy.wait()


def decode_kernel(
    dec_rows,
    grid_hbm,
    w_hbm,
    dec_table_hbm,
    apart_hbm,
    grid_dst_hbm,
    grid_self_hbm,
    mesh_hbm,
    grid_out_hbm,
    mesh_out_hbm,
    grid_ref,
    w_ref,
    dec_table,
    apart,
    grid_dst,
    grid_self,
    out_buf,
    in_sem,
    out_sem,
):
    grid_rows, width = grid_ref.shape
    step = grid_rows
    loads = [
        pltpu.make_async_copy(src, dst, in_sem.at[i])
        for i, (src, dst) in enumerate(
            [
                (dec_table_hbm, dec_table),
                (apart_hbm, apart),
                (grid_dst_hbm, grid_dst),
                (w_hbm.at[2, 2], w_ref.at[0]),
                (w_hbm.at[2, 4], w_ref.at[1]),
                (grid_self_hbm, grid_self),
                (w_hbm.at[2, 5], w_ref.at[2]),
                (grid_hbm, grid_ref),
                (mesh_hbm, mesh_out_hbm),
            ]
        )
    ]
    for load in loads:
        load.start()
    for load in loads[:4]:
        load.wait()
    row_id = lax.broadcasted_iota(jnp.int32, (dec_rows, 128), 0).astype(F32)
    rest = jnp.zeros((128 - dec_rows - 12, 128), F32)
    out_copies = []
    for i in range(0, grid_rows, step):
        dec_agg = jnp.zeros((step, width), F32)
        for t in range(3):
            pieces = []
            for q in range(i // 128, (i + step) // 128):
                info = apart[q * 16 : (q + 1) * 16, t * 128 : (t + 1) * 128]
                high, low = info[1:5], info[5:9]
                pieces.append(
                    jnp.concatenate(
                        [(row_id == info[0:1]).astype(F32), high, low, high, rest], axis=0
                    ).astype(BF)
                )
            pre = dot_t(jnp.concatenate(pieces, axis=1), dec_table[...]) + grid_dst[
                pl.ds(i, step), :
            ].astype(F32)
            message = layer_norm(dot(silu(pre), w_ref[0])).astype(BF)
            dec_agg = dec_agg + message.astype(F32)
        if i == 0:
            loads[4].wait()
            loads[5].wait()
        hidden = silu(grid_self[pl.ds(i, step), :].astype(F32) + dot(dec_agg.astype(BF), w_ref[1]))
        if i == 0:
            loads[6].wait()
            loads[7].wait()
        out_buf[pl.ds(i, step), :] = (
            grid_ref[pl.ds(i, step), :].astype(F32) + layer_norm(dot(hidden, w_ref[2]))
        ).astype(BF)
        copy = pltpu.make_async_copy(
            out_buf.at[pl.ds(i, step), :], grid_out_hbm.at[pl.ds(i, step), :], out_sem.at[i // step]
        )
        copy.start()
        out_copies.append(copy)
    loads[8].wait()
    for copy in out_copies:
        copy.wait()


def shards(
    grid_nodes,
    mesh_nodes,
    weights,
    raw_weights,
    enc_raw,
    enc_src,
    enc_dst,
    enc_count,
    enc_send,
    proc_raw,
    proc_src,
    proc_dst,
    proc_count,
    proc_send,
    dec_raw,
    dec_src,
    dec_send,
):
    n = lax.axis_size("band")
    grid_rows, width = grid_nodes.shape
    mesh_rows = mesh_nodes.shape[0]
    cap_g = enc_send.shape[1] // 2
    cap_d = dec_send.shape[1] // 2
    near = proc_send.shape[2]
    far_rows = -(-(mesh_rows + 2 * near + 2 * n) // 128) * 128
    smalls = (
        mesh_nodes, raw_weights, enc_raw, enc_src, enc_dst, enc_send,
        proc_raw, proc_src, proc_dst, proc_send, dec_raw, dec_src, dec_send,
    )
    hbm = pl.BlockSpec(memory_space=pl.ANY)
    smem = pl.BlockSpec(memory_space=pltpu.SMEM)
    dec_table, apart, grid_dst, grid_self, mesh_out = pl.pallas_call(
        functools.partial(exchange_kernel, n, far_rows),
        out_shape=(
            jax.ShapeDtypeStruct((128, width), BF),
            jax.ShapeDtypeStruct((grid_rows // 8, 384), F32),
            jax.ShapeDtypeStruct(grid_nodes.shape, BF),
            jax.ShapeDtypeStruct(grid_nodes.shape, BF),
            jax.ShapeDtypeStruct(mesh_nodes.shape, BF),
        ),
        in_specs=[hbm] * 7 + [smem] + [hbm] * 4 + [smem] + [hbm] * 4,
        out_specs=(hbm,) * 5,
        scratch_shapes=[
            pltpu.VMEM((grid_rows, width), BF),
            pltpu.VMEM(weights.shape, BF),
            pltpu.VMEM((2 * cap_g + grid_rows + 128, width), BF),
            pltpu.VMEM((2 * cap_g, width), BF),
            pltpu.VMEM((enc_src.shape[0], width), F32),
            pltpu.VMEM((far_rows + 128, width), BF),
            pltpu.VMEM((2 * near, width), BF),
            pltpu.VMEM((8 * n, 128), F32),
            pltpu.VMEM((8 * n, 128), F32),
            pltpu.VMEM((128, width), BF),
            pltpu.VMEM((2 * cap_d, width), BF),
            pltpu.VMEM((grid_rows // 8, 384), F32),
            pltpu.VMEM((grid_rows, width), BF),
            pltpu.VMEM((grid_rows, width), BF),
            pltpu.VMEM(mesh_nodes.shape, BF),
            pltpu.SemaphoreType.DMA(weights.shape[:2]),
            pltpu.SemaphoreType.DMA,
            pltpu.SemaphoreType.DMA((7,)),
            pltpu.SemaphoreType.DMA((6,)),
            pltpu.SemaphoreType.DMA((6,)),
            pltpu.SemaphoreType.DMA((n,)),
            pltpu.SemaphoreType.DMA((n,)),
            *(pltpu.VMEM(small.shape, small.dtype) for small in smalls),
            pltpu.SemaphoreType.DMA((len(smalls),)),
        ],
        compiler_params=pltpu.CompilerParams(
            collective_id=0, has_side_effects=True, vmem_limit_bytes=56 * 2**20
        ),
    )(
        grid_nodes, mesh_nodes, weights, raw_weights,
        enc_raw, enc_src, enc_dst, enc_count, enc_send,
        proc_raw, proc_src, proc_dst, proc_count, proc_send,
        dec_raw, dec_src, dec_send,
    )
    return pl.pallas_call(
        functools.partial(decode_kernel, mesh_rows + 2 * cap_d),
        out_shape=(
            jax.ShapeDtypeStruct(grid_nodes.shape, BF),
            jax.ShapeDtypeStruct(mesh_nodes.shape, BF),
        ),
        in_specs=[hbm] * 7,
        out_specs=(hbm, hbm),
        scratch_shapes=[
            pltpu.VMEM((grid_rows, width), BF),
            pltpu.VMEM((3, width, width), BF),
            pltpu.VMEM((128, width), BF),
            pltpu.VMEM((grid_rows // 8, 384), F32),
            pltpu.VMEM((grid_rows, width), BF),
            pltpu.VMEM((grid_rows, width), BF),
            pltpu.VMEM((grid_rows, width), BF),
            pltpu.SemaphoreType.DMA((9,)),
            pltpu.SemaphoreType.DMA((1,)),
        ],
        compiler_params=pltpu.CompilerParams(vmem_limit_bytes=56 * 2**20),
    )(grid_nodes, weights, dec_table, apart, grid_dst, grid_self, mesh_out)


def solution(mesh):
    placed = (
        P(("parts", "band"), None),
        P(("parts", "band"), None),
        P(),
        P(),
        P(None, "band"),
        P("band"),
        P("band"),
        P("band"),
        P("band", None),
        P(None, "band"),
        P("band"),
        P("band"),
        P("band"),
        P("band", None, None),
        P(None, "band"),
        P("band"),
        P("band", None),
    )
    return jax.shard_map(
        shards,
        mesh=mesh,
        in_specs=placed,
        out_specs=(P(("parts", "band"), None), P(("parts", "band"), None)),
        check_vma=False,
    )
```
